32 devices in a mesh: ctx: 16 (over z, y, core), head: 2 (over x).
Axes of the slice: x: 2, y: 2, z: 4, core: 2. Of those that a mesh axis runs over, the one named last changes fastest.
Arguments:
- latent_raw: bfloat16 [2048, 576], P(('ctx', 'head')), may hold values from -6 to 6
- kv_gain: float32 [512], replicated, may hold values from 0.1 to 1.9
- query_nope: bfloat16 [2048, 8192], P('ctx', 'head'), may hold values from -144 to 144
- query_rope: bfloat16 [2048, 4096], P('ctx', 'head'), may hold values from -6 to 6
- key_up: bfloat16 [64, 128, 512], P('head'), may hold values from -0.5 to 0.5
- value_up: bfloat16 [64, 512, 128], P('head'), may hold values from -0.25 to 0.25
- doc_lengths: int32 [4], replicated, may hold values from 1 to 896, 2048 in all
Outputs:
- attended: bfloat16 [2048, 8192], P('ctx', 'head')
The draws below stay inside these ranges and needn't reach their ends.
Inputs may be any that keep to these rules, and one draw needn't show every extreme that they name: `doc_lengths`: documents lie end to end over all 2048 positions; the longest has exactly 896 positions.
All inputs are finite; a program needn't handle non-finite values.
Results may differ from the reference program's by a relative error of at most 0.012.
The reference program's roundings to bfloat16 on the way (of `kv_rows`, `absorbed`, `rotated`, `weights` and `mixed_latent`) count: a program that leaves them out, or rounds other values in their place, can miss the bound.
Values may be sent and summed in bfloat16 or wider, within the bound.
No kernel may reach another device: no remote copies, remote signals or barrier semaphores. Data moves between devices by JAX's collectives and lax.ppermute only.
A program may use at most 64 MiB of HBM per device.

```python
import math
import jax
import jax.numpy as jnp
import numpy as np
from jax import lax

KV_RANK = 512
ROPE = 64
NOPE = 128
VDIM = 128
HEADS = 64
TOK_DEV = 128
HOPS = 7
TOKENS = 2048
MOST = 896
DOCS = 4
N_CTX = 16


def draw_query_nope(key, part):
    key_base = jax.random.fold_in(key, 0)
    base = jnp.clip(jax.random.normal(key_base, (TOKENS, HEADS * NOPE), jnp.float32), -6.0, 6.0)
    return (0.7 * base).astype(jnp.bfloat16)


def levels(own_key, shape, shards, least, high):
    def one(axis_at, shards_of):
        draws = jax.random.uniform(jax.random.fold_in(jax.random.fold_in(own_key, 6), axis_at), (shards_of,), jnp.float32, least / len(shards), high / len(shards))
        return jnp.repeat(jnp.exp(draws), shape[axis_at] // shards_of).reshape((-1,) + (1,) * (len(shape) - axis_at - 1))

    level = one(*shards[0])
    for cut in shards[1:]:
        level = level * one(*cut)
    return level


def length_profile(number_of, total, reach, skew):
    loads = [(1 << 20) // math.isqrt(rank ** skew) + 1 for rank in range(2, number_of + 1)]
    spare, given = total - reach - (number_of - 1), [1] * (number_of - 1)
    while spare > 0:
        movable = [i for i in range(number_of - 1) if given[i] < reach]
        whole, budget = sum([loads[i] for i in movable]), spare
        for i in movable:
            addition = min(reach - given[i], max(1, budget * loads[i] // whole), spare)
            given[i] = given[i] + addition
            spare = spare - addition
    return np.array([reach] + given)


def uneven_parts(key, count, total, most, slope):
    if count == 2:
        one = jax.random.randint(key, (), max(1, total - most), min(most, total - 1) + 1)
        return jnp.stack([one, total - one])
    sizes = jnp.asarray(length_profile(count, total, most, slope), jnp.int32)
    pairs = (count - 1) // 2
    giver, taker = sizes[1:1 + 2 * pairs:2], sizes[2:2 + 2 * pairs:2]
    room = jnp.minimum(giver - 1, most - taker)
    moved = jax.random.randint(jax.random.fold_in(key, 1), (pairs,), 0, 1 << 20) % (room + 1)
    sizes = sizes.at[1:1 + 2 * pairs:2].set(giver - moved).at[2:2 + 2 * pairs:2].set(taker + moved)
    return sizes[jax.random.permutation(jax.random.fold_in(key, 2), count)]


def normal_values(own_key, dims, scale, most, cuts=(), held_as=jnp.bfloat16):
    array = scale * jax.random.normal(own_key, dims, jnp.float32)
    if cuts:
        array = array * levels(own_key, dims, cuts, -0.22, 0.18)
    return jnp.clip(array, -most, most).astype(held_as)


def setup_inputs(seed: int = 0) -> dict:
    seeds = jax.random.split(jax.random.key(seed), 8)
    return {
        "latent_raw": normal_values(seeds[0], (TOKENS, KV_RANK + ROPE), 1.0, 6.0, ((0, 32),)),
        "kv_gain": jnp.clip(1.0 + 0.18 * jax.random.normal(seeds[1], (KV_RANK,), jnp.float32), 0.1, 1.9),
        "query_nope": draw_query_nope(jax.random.fold_in(seeds[7], 71), 0),
        "query_rope": normal_values(seeds[3], (TOKENS, HEADS * ROPE), 1.0, 6.0, ((0, 16), (1, 2))),
        "key_up": normal_values(seeds[4], (HEADS, NOPE, KV_RANK), NOPE ** -0.5, 0.5, ((0, 2),)),
        "value_up": normal_values(seeds[5], (HEADS, KV_RANK, VDIM), KV_RANK ** -0.5, 0.25, ((0, 2),)),
        "doc_lengths": uneven_parts(seeds[6], DOCS, TOKENS, MOST, 2).astype(jnp.int32),
    }


epsilon = 1e-06
masked_score = -1e+30

def doc_begin(positions, starts):
    inside = starts[None, :] <= positions[:, None]
    return lax.optimization_barrier(jnp.max(jnp.where(inside, starts[None, :], 0), axis=1)).astype(jnp.int32)

def rotation(offsets, rope_half):
    frequency = 10000.0 ** (-2.0 * jnp.arange(rope_half, dtype=jnp.float32) / (2 * rope_half))
    angles = offsets.astype(jnp.float32)[:, None] * frequency[None, :]
    return (jnp.cos(angles), jnp.sin(angles))

def rotate(values, cos_table, sin_table):
    rope_half = cos_table.shape[-1]
    first_half = values[..., :rope_half]
    second_half = values[..., rope_half:]
    return jnp.concatenate([first_half * cos_table - second_half * sin_table, second_half * cos_table + first_half * sin_table], axis=-1)

def reference(latent_raw, kv_gain, query_nope, query_rope, key_up, value_up, doc_lengths):
    score_scale = (NOPE + ROPE) ** (-0.5)
    starts = (jnp.cumsum(doc_lengths) - doc_lengths).astype(jnp.int32)
    positions = jnp.arange(TOKENS, dtype=jnp.int32)
    begins = doc_begin(positions, starts)
    cos_table, sin_table = rotation(positions - begins, ROPE // 2)
    raw_rows = latent_raw.astype(jnp.float32)
    latent_part = raw_rows[:, :KV_RANK]
    normed = latent_part * lax.rsqrt(lax.optimization_barrier(jnp.mean(latent_part * latent_part, axis=1, keepdims=True)) + epsilon) * kv_gain
    kv_rows = jnp.concatenate([normed, rotate(raw_rows[:, KV_RANK:], cos_table, sin_table)], axis=1).astype(jnp.bfloat16)
    span_rows = (HOPS + 1) * TOK_DEV
    pad_rows = HOPS * TOK_DEV
    kv_padded = jnp.concatenate([jnp.zeros((pad_rows, KV_RANK + ROPE), jnp.bfloat16), kv_rows], axis=0)
    kv_padded = lax.optimization_barrier(kv_padded).astype(jnp.float32)
    begin_padded = jnp.concatenate([jnp.full((pad_rows,), -1, jnp.int32), begins], axis=0)
    key_weight = key_up.astype(jnp.float32)
    value_weight = value_up.astype(jnp.float32)

    def query_block(block_index):
        first_row = (block_index * TOK_DEV).astype(jnp.int32)
        query_pos = first_row + jnp.arange(TOK_DEV, dtype=jnp.int32)
        query_begin = lax.dynamic_slice_in_dim(begins, first_row, TOK_DEV, 0)
        nope_rows = lax.dynamic_slice_in_dim(query_nope, first_row, TOK_DEV, 0).astype(jnp.float32).reshape(TOK_DEV, HEADS, NOPE)
        absorbed = jnp.einsum('thn,hnr->thr', nope_rows, key_weight).astype(jnp.bfloat16)
        rope_rows = lax.dynamic_slice_in_dim(query_rope, first_row, TOK_DEV, 0).astype(jnp.float32).reshape(TOK_DEV, HEADS, ROPE)
        cos_query = lax.dynamic_slice_in_dim(cos_table, first_row, TOK_DEV, 0)
        sin_query = lax.dynamic_slice_in_dim(sin_table, first_row, TOK_DEV, 0)
        rotated = rotate(rope_rows, cos_query[:, None, :], sin_query[:, None, :]).astype(jnp.bfloat16)
        queries = lax.optimization_barrier(jnp.concatenate([absorbed, rotated], axis=2)).astype(jnp.float32)
        key_rows = lax.dynamic_slice_in_dim(kv_padded, first_row, span_rows, 0)
        key_begin = lax.dynamic_slice_in_dim(begin_padded, first_row, span_rows, 0)
        key_pos = first_row - pad_rows + jnp.arange(span_rows, dtype=jnp.int32)
        live_pairs = (key_pos[None, :] <= query_pos[:, None]) & (key_begin[None, :] == query_begin[:, None])
        scores = jnp.einsum('thc,sc->hts', queries, key_rows) * score_scale
        scores = jnp.where(live_pairs[None], scores, masked_score)
        row_max = lax.optimization_barrier(jnp.max(scores, axis=2, keepdims=True))
        weights = jnp.where(live_pairs[None], jnp.exp(scores - row_max), 0.0)
        totals = lax.optimization_barrier(jnp.sum(weights, axis=2))
        rounded = lax.optimization_barrier(weights.astype(jnp.bfloat16)).astype(jnp.float32)
        mixed_latent = (jnp.einsum('hts,sr->htr', rounded, key_rows[:, :KV_RANK]) / totals[:, :, None]).astype(jnp.bfloat16)
        mixed_latent = lax.optimization_barrier(mixed_latent).astype(jnp.float32)
        attended = jnp.einsum('htr,hrv->thv', mixed_latent, value_weight)
        return attended.astype(jnp.bfloat16).reshape(TOK_DEV, HEADS * VDIM)
    blocks = lax.map(query_block, jnp.arange(N_CTX, dtype=jnp.int32))
    return blocks.reshape(TOKENS, HEADS * VDIM)
```

```python
import functools

import jax
import jax.numpy as jnp
import numpy as np
from jax import lax
from jax.experimental import pallas as pl
from jax.experimental.pallas import tpu as pltpu
from jax.sharding import PartitionSpec as P

epsilon = 1e-06
masked_score = -1e30
PLANE = 4
GROUP = 8
SUB = 4
VMEM = pl.BlockSpec(memory_space=pltpu.VMEM)
SMEM = pl.BlockSpec(memory_space=pltpu.SMEM)


def begin_of(positions, lengths_ref):
    begin = jnp.zeros_like(positions)
    start = jnp.int32(0)
    for doc in range(lengths_ref.shape[0] - 1):
        start = start + lengths_ref[doc]
        begin = jnp.where(positions >= start, start, begin)
    return begin


def half_start(plane, flip_y, flip_core, flip_head, block_rows, half_rows):
    ctx = lax.axis_index("ctx")
    head = lax.axis_index("head")
    core = lax.rem(ctx, 2)
    row = lax.rem(ctx // 2, 2)
    base = ctx // PLANE - plane
    row = 1 - row if flip_y else row
    core = 1 - core if flip_core else core
    head = 1 - head if flip_head else head
    return (base * PLANE + row * 2 + core) * block_rows + head * half_rows


def query_kernel(lengths_ref, freq_ref, qn_ref, qr_ref, ku_ref, q_ref, cos_ref, sin_ref):
    rows = qn_ref.shape[0]
    heads, nope, latent = ku_ref.shape
    rope = qr_ref.shape[1] // heads
    ctx = lax.axis_index("ctx")
    freq = freq_ref[0:1, :]
    key_rows = rows // 2
    for plane in range(3):
        first = half_start(plane, False, False, False, rows, key_rows)
        pos = first + lax.broadcasted_iota(jnp.int32, (key_rows, 128), 0)
        angle = (pos - begin_of(pos, lengths_ref)).astype(jnp.float32) * freq
        cos_ref[plane] = jnp.cos(angle)
        sin_ref[plane] = jnp.sin(angle)
    pos = ctx * rows + lax.broadcasted_iota(jnp.int32, (rows, 128), 0)
    angle = (pos - begin_of(pos, lengths_ref)).astype(jnp.float32) * freq
    lane = lax.broadcasted_iota(jnp.int32, (rows, 128), 1)
    low = lax.rem(lane, rope) < rope // 2
    cos = jnp.cos(angle)
    sin = jnp.sin(angle)
    sin = jnp.where(low, -sin, sin)

    def group(index, carry):
        for j in range(0, GROUP, 2):
            head = index * GROUP + j
            pair = qr_ref[:, pl.ds(pl.multiple_of(head * rope, 128), 128)].astype(jnp.float32)
            partner = jnp.where(low, pltpu.roll(pair, 128 - rope // 2, 1), pltpu.roll(pair, rope // 2, 1))
            rotated = pair * cos + partner * sin
            shifted = pltpu.roll(rotated, rope, 1)
            for k in range(2):
                at = pl.ds(pl.multiple_of((head + k) * rows, rows), rows)
                nope_rows = qn_ref[:, pl.ds(pl.multiple_of((head + k) * nope, 128), nope)]
                absorbed = jnp.dot(nope_rows, ku_ref[head + k], preferred_element_type=jnp.float32)
                q_ref[at, :latent] = absorbed.astype(jnp.bfloat16)
                part = rotated if k == 0 else shifted
                q_ref[at, latent:] = jnp.where(lane < rope, part, 0.0).astype(jnp.bfloat16)
        return carry

    lax.fori_loop(0, heads // GROUP, group, 0)


def rows_kernel(own_ref, one_ref, two_ref, gain_ref, cos_ref, sin_ref, rows_ref, send_ref):
    latent = gain_ref.shape[1]
    full = own_ref.shape[1]
    half = (full - latent) // 2
    row = lax.rem(lax.axis_index("ctx") // 2, 2)
    gain = gain_ref[0:1, :]
    for plane, raw_ref in enumerate((own_ref, one_ref, two_ref)):
        part = raw_ref[:, :latent].astype(jnp.float32)
        mean = jnp.mean(part * part, axis=1, keepdims=True)
        normed = part * lax.rsqrt(mean + epsilon) * gain
        rope = raw_ref[:, latent:].astype(jnp.float32)
        first, second = rope[:, :half], rope[:, half:]
        cos, sin = cos_ref[plane][:, :half], sin_ref[plane][:, :half]
        turned = jnp.concatenate([first * cos - second * sin, second * cos + first * sin], axis=1)
        rows_ref[plane, :, :latent] = normed.astype(jnp.bfloat16)
        rows_ref[plane, :, latent:] = turned.astype(jnp.bfloat16)
    send_ref[...] = rows_ref[pl.ds(row, 2)]


def attend_kernel(layout, scale, lengths_ref, q_ref, vu_ref, *refs):
    count = len(layout)
    piece_refs = refs[:count]
    out_ref, kv_ref = refs[count:]
    heads, latent, value = vu_ref.shape
    rows = q_ref.shape[0] // heads
    half_rows = rows // 2
    ctx = lax.axis_index("ctx")
    core = lax.rem(ctx, 2)
    row = lax.rem(ctx // 2, 2)
    keys = kv_ref.shape[0]
    full = piece_refs[0].shape[2]
    kv_ref[:, full:] = jnp.zeros((keys, kv_ref.shape[1] - full), jnp.bfloat16)
    lane = lax.broadcasted_iota(jnp.int32, (rows, keys), 1)
    key_pos = jnp.zeros((rows, keys), jnp.int32)
    at = 0
    for (flip_y, flip_core, flip_head), ref in zip(layout, piece_refs):
        if flip_y:
            index, plane = 0, 1 - row
        else:
            index = plane = 1 - core if flip_core else 0
        for step in range(2):
            kv_ref[at : at + half_rows, :full] = ref[index + step]
            first = half_start(plane + step, flip_y, flip_core, flip_head, rows, half_rows)
            key_pos = jnp.where(lane >= at, first + lane - at, key_pos)
            at += half_rows
    pos = ctx * rows + lax.broadcasted_iota(jnp.int32, (rows, keys), 0)
    live = (key_pos <= pos) & (key_pos >= begin_of(pos, lengths_ref))

    def scores(base):
        at = pl.ds(pl.multiple_of(base * rows, rows), SUB * rows)
        return lax.dot_general(
            q_ref[at, :], kv_ref[...], (((1,), (1,)), ((), ())), preferred_element_type=jnp.float32
        )

    def group(index, carry):
        subs = GROUP // SUB
        now = scores(index * GROUP)
        for sub in range(subs):
            base = index * GROUP + sub * SUB
            later = scores(base + SUB) if sub + 1 < subs else None
            now = jnp.where(live[None], now.reshape(SUB, rows, keys) * scale, masked_score)
            most = jnp.max(now, axis=2, keepdims=True)
            weights = jnp.exp(now - most)
            total = jnp.sum(weights, axis=2, keepdims=True).reshape(SUB * rows, 1)
            mixed = jnp.dot(
                weights.astype(jnp.bfloat16).reshape(SUB * rows, keys),
                kv_ref[:, :latent],
                preferred_element_type=jnp.float32,
            )
            mixed = (mixed / total).astype(jnp.bfloat16)
            for j in range(SUB):
                result = jnp.dot(
                    mixed[j * rows : (j + 1) * rows], vu_ref[base + j], preferred_element_type=jnp.float32
                )
                out_ref[:, pl.ds(pl.multiple_of((base + j) * value, 128), value)] = result.astype(jnp.bfloat16)
            now = later
        return carry

    lax.fori_loop(0, heads // GROUP, group, 0)


def params():
    return pltpu.CompilerParams(vmem_limit_bytes=48 * 2**20)


def shards(latent_raw, kv_gain, query_nope, query_rope, key_up, value_up, doc_lengths):
    rows = query_nope.shape[0]
    heads, nope, latent = key_up.shape
    value = value_up.shape[2]
    half_rows, full = latent_raw.shape
    rope = full - latent
    wide = latent + 128
    ctx_size = lax.axis_size("ctx")
    scale = (nope + rope) ** (-0.5)

    def plane_shift(array, planes):
        steps = planes * PLANE
        return lax.ppermute(array, "ctx", [(s, (s + steps) % ctx_size) for s in range(ctx_size)])

    def swap_ctx(array, bit):
        return lax.ppermute(array, "ctx", [(s, s ^ bit) for s in range(ctx_size)])

    def swap_head(array):
        return lax.ppermute(array, "head", [(0, 1), (1, 0)])

    one = plane_shift(latent_raw, 1)
    two = plane_shift(latent_raw, 2)
    freq = np.float32(10000.0) ** (np.float32(-2.0) * np.arange(rope // 2, dtype=np.float32) / np.float32(rope))
    freq = jnp.asarray(np.tile(freq.astype(np.float32), (8, 128 // (rope // 2))))
    table = jax.ShapeDtypeStruct((3, half_rows, 128), jnp.float32)
    queries, cos, sin = pl.pallas_call(
        query_kernel,
        out_shape=(jax.ShapeDtypeStruct((heads * rows, wide), jnp.bfloat16), table, table),
        in_specs=[SMEM] + [VMEM] * 4,
        out_specs=[VMEM] * 3,
        compiler_params=params(),
        cost_estimate=pl.CostEstimate(
            flops=2 * heads * rows * nope * latent, bytes_accessed=8 * 2**20, transcendentals=0
        ),
        name="queries",
    )(doc_lengths, freq, query_nope, query_rope, key_up)
    near, send = pl.pallas_call(
        rows_kernel,
        out_shape=(
            jax.ShapeDtypeStruct((3, half_rows, full), jnp.bfloat16),
            jax.ShapeDtypeStruct((2, half_rows, full), jnp.bfloat16),
        ),
        in_specs=[VMEM] * 6,
        out_specs=[VMEM] * 2,
        compiler_params=params(),
        name="rows",
    )(latent_raw, one, two, kv_gain[None], cos, sin)
    across = swap_ctx(send, 2)
    side = swap_head(near)
    corner = swap_head(across)
    pieces = [near, across, side, corner]
    pieces = pieces + [swap_ctx(piece, 1) for piece in pieces]
    layout = []
    for flip_core in (False, True):
        layout += [(False, flip_core, False), (True, flip_core, False), (False, flip_core, True), (True, flip_core, True)]
    keys = 2 * half_rows * len(pieces)
    return pl.pallas_call(
        functools.partial(attend_kernel, tuple(layout), scale),
        out_shape=jax.ShapeDtypeStruct((rows, heads * value), jnp.bfloat16),
        in_specs=[SMEM] + [VMEM] * (2 + len(pieces)),
        out_specs=VMEM,
        scratch_shapes=[pltpu.VMEM((keys, wide), jnp.bfloat16)],
        compiler_params=params(),
        name="attend",
    )(doc_lengths, queries, value_up, *pieces)


def solution(mesh):
    return jax.shard_map(
        shards,
        mesh=mesh,
        in_specs=(
            P(("ctx", "head"), None),
            P(),
            P("ctx", "head"),
            P("ctx", "head"),
            P("head", None, None),
            P("head", None, None),
            P(),
        ),
        out_specs=P("ctx", "head"),
        check_vma=False,
    )
```

```python
import functools
import math

import jax
import jax.numpy as jnp
import numpy as np
from jax import lax
from jax.experimental import pallas as pl
from jax.experimental.pallas import tpu as pltpu
from jax.sharding import PartitionSpec as P

epsilon = 1e-06
masked_score = -1e30
PLANE = 4
GROUP = 8
SPAN = 32
SUB = 4
VALUE_GROUP = 32
HBM = pl.BlockSpec(memory_space=pltpu.HBM)
VMEM = pl.BlockSpec(memory_space=pltpu.VMEM)
SMEM = pl.BlockSpec(memory_space=pltpu.SMEM)


def begin_of(positions, lengths_ref):
    begin = jnp.zeros_like(positions)
    start = jnp.int32(0)
    for doc in range(lengths_ref.shape[0] - 1):
        start = start + lengths_ref[doc]
        begin = jnp.where(positions >= start, start, begin)
    return begin


def half_start(plane, flip_y, flip_core, flip_head, block_rows, half_rows):
    ctx = lax.axis_index("ctx")
    head = lax.axis_index("head")
    core = lax.rem(ctx, 2)
    row = lax.rem(ctx // 2, 2)
    base = ctx // PLANE - plane
    row = 1 - row if flip_y else row
    core = 1 - core if flip_core else core
    head = 1 - head if flip_head else head
    return (base * PLANE + row * 2 + core) * block_rows + head * half_rows


def frequencies(rope, shape):
    half = rope // 2
    exponents = np.float32(-2.0) * np.arange(half, dtype=np.float32) / np.float32(rope)
    values = np.float32(10000.0) ** exponents
    lane = lax.rem(lax.broadcasted_iota(jnp.int32, shape, 1), half)
    freq = jnp.zeros(shape, jnp.float32)
    for index in range(half):
        freq = jnp.where(lane == index, float(values[index]), freq)
    return freq


def query_kernel(lengths_hbm, qn_hbm, qr_hbm, ku_hbm, q_ref, cos_ref, sin_ref, qn_ref, qr_ref, ku_ref, lengths_ref, sems):
    rows = qn_ref.shape[0]
    heads, nope, latent = ku_ref.shape
    rope = qr_ref.shape[1] // heads
    groups = heads // GROUP

    def copies(index):
        head = index * GROUP
        cols = pl.ds(head * nope, GROUP * nope)
        part = pl.ds(head, GROUP)
        return [
            pltpu.make_async_copy(qn_hbm.at[:, cols], qn_ref.at[:, cols], sems.at[index, 0]),
            pltpu.make_async_copy(ku_hbm.at[part], ku_ref.at[part], sems.at[index, 1]),
        ]

    rope_copy = pltpu.make_async_copy(qr_hbm, qr_ref, sems.at[groups, 0])
    lengths_copy = pltpu.make_async_copy(lengths_hbm, lengths_ref, sems.at[groups, 1])
    lengths_copy.start()
    rope_copy.start()
    for index in range(groups):
        for copy in copies(index):
            copy.start()
    lengths_copy.wait()
    ctx = lax.axis_index("ctx")
    freq = frequencies(rope, (8, 128))[0:1, :]
    key_rows = rows // 2
    for plane in range(3):
        first = half_start(plane, False, False, False, rows, key_rows)
        pos = first + lax.broadcasted_iota(jnp.int32, (key_rows, 128), 0)
        angle = (pos - begin_of(pos, lengths_ref)).astype(jnp.float32) * freq
        cos_ref[plane] = jnp.cos(angle)
        sin_ref[plane] = jnp.sin(angle)
    pos = ctx * rows + lax.broadcasted_iota(jnp.int32, (rows, 128), 0)
    angle = (pos - begin_of(pos, lengths_ref)).astype(jnp.float32) * freq
    lane = lax.broadcasted_iota(jnp.int32, (rows, 128), 1)
    low = lax.rem(lane, rope) < rope // 2
    cos = jnp.cos(angle)
    sin = jnp.sin(angle)
    sin = jnp.where(low, -sin, sin)
    rope_copy.wait()
    for index in range(groups):
        for copy in copies(index):
            copy.wait()
        for head in range(index * GROUP, (index + 1) * GROUP, 2):
            pair = qr_ref[:, head * rope : (head + 2) * rope].astype(jnp.float32)
            partner = jnp.where(low, pltpu.roll(pair, 128 - rope // 2, 1), pltpu.roll(pair, rope // 2, 1))
            rotated = pair * cos + partner * sin
            for k, part in enumerate((rotated, pltpu.roll(rotated, rope, 1))):
                at = slice((head + k) * rows, (head + k + 1) * rows)
                nope_rows = qn_ref[:, (head + k) * nope : (head + k + 1) * nope]
                absorbed = jnp.dot(nope_rows, ku_ref[head + k], preferred_element_type=jnp.float32)
                q_ref[at, :latent] = absorbed.astype(jnp.bfloat16)
                q_ref[at, latent:] = jnp.where(lane < rope, part, 0.0).astype(jnp.bfloat16)


def rows_kernel(own_ref, one_ref, two_ref, gain_ref, cos_ref, sin_ref, rows_ref, send_ref):
    latent = gain_ref.shape[1]
    full = own_ref.shape[1]
    half = (full - latent) // 2
    row = lax.rem(lax.axis_index("ctx") // 2, 2)
    gain = gain_ref[0:1, :]
    for plane, raw_ref in enumerate((own_ref, one_ref, two_ref)):
        part = raw_ref[:, :latent].astype(jnp.float32)
        mean = jnp.mean(part * part, axis=1, keepdims=True)
        normed = part * lax.rsqrt(mean + epsilon) * gain
        rope = raw_ref[:, latent:].astype(jnp.float32)
        first, second = rope[:, :half], rope[:, half:]
        cos, sin = cos_ref[plane][:, :half], sin_ref[plane][:, :half]
        turned = jnp.concatenate([first * cos - second * sin, second * cos + first * sin], axis=1)
        rows_ref[plane, :, :latent] = normed.astype(jnp.bfloat16)
        rows_ref[plane, :, latent:] = turned.astype(jnp.bfloat16)
    send_ref[...] = rows_ref[pl.ds(row, 2)]


def widen(column, count):
    return jnp.concatenate([column] * count, axis=1)


def value_heads(mixed_ref, vu_ref, out_ref):
    heads, latent, value = vu_ref.shape
    rows = out_ref.shape[0]

    def group(index, carry):
        for j in range(VALUE_GROUP):
            head = index * VALUE_GROUP + j
            at = pl.ds(pl.multiple_of(head * rows, rows), rows)
            result = jnp.dot(mixed_ref[at, :], vu_ref[head], preferred_element_type=jnp.float32)
            out_ref[:, pl.ds(pl.multiple_of(head * value, 128), value)] = result.astype(jnp.bfloat16)
        return carry

    lax.fori_loop(0, heads // VALUE_GROUP, group, 0)


def attend_kernel(layout, scale, first_call, last_call, lengths_ref, q_ref, *refs):
    count = len(layout)
    piece_refs, refs = refs[:count], refs[count:]
    if not first_call:
        sum_in, most_in, total_in = refs[:3]
        refs = refs[3:]
    if last_call:
        vu_ref, out_ref, mixed_ref, kv_ref = refs
        latent = mixed_ref.shape[1]
    else:
        sum_out, most_out, total_out, kv_ref = refs
        latent = sum_out.shape[1]
    half_rows = piece_refs[0].shape[1]
    rows = 2 * half_rows
    heads = q_ref.shape[0] // rows
    ctx = lax.axis_index("ctx")
    core = lax.rem(ctx, 2)
    row = lax.rem(ctx // 2, 2)
    keys = kv_ref.shape[0]
    full = piece_refs[0].shape[2]
    kv_ref[:, full:] = jnp.zeros((keys, kv_ref.shape[1] - full), jnp.bfloat16)
    lane = lax.broadcasted_iota(jnp.int32, (rows, keys), 1)
    key_pos = jnp.zeros((rows, keys), jnp.int32)
    at = 0
    for (flip_y, flip_core, flip_head), ref in zip(layout, piece_refs):
        if flip_y:
            index, plane = 0, 1 - row
        else:
            index = plane = 1 - core if flip_core else 0
        for step in range(2):
            kv_ref[at : at + half_rows, :full] = ref[index + step]
            first = half_start(plane + step, flip_y, flip_core, flip_head, rows, half_rows)
            key_pos = jnp.where(lane >= at, first + lane - at, key_pos)
            at += half_rows
    pos = ctx * rows + lax.broadcasted_iota(jnp.int32, (rows, keys), 0)
    live = (key_pos <= pos) & (key_pos >= begin_of(pos, lengths_ref))

    exponent = scale * math.log2(math.e)

    def span(base):
        return pl.ds(pl.multiple_of(base * rows, rows), SUB * rows)

    def scores(base):
        return lax.dot_general(
            q_ref[span(base), :], kv_ref[...], (((1,), (1,)), ((), ())), preferred_element_type=jnp.float32
        )

    def group(index, carry):
        subs = SPAN // SUB
        now = scores(index * SPAN)
        for sub in range(subs):
            base = index * SPAN + sub * SUB
            later = scores(base + SUB) if sub + 1 < subs else None
            now = jnp.where(live[None], now.reshape(SUB, rows, keys), masked_score)
            now = now.reshape(SUB * rows, keys)
            most = jnp.broadcast_to(jnp.max(now, axis=1, keepdims=True), (SUB * rows, 128))
            if not first_call:
                before = most_in[span(base), :]
                most = jnp.maximum(most, before)
                factor = jnp.exp2((before - most) * exponent)
            weights = jnp.exp2((now - widen(most, keys // 128)) * exponent)
            total = jnp.broadcast_to(jnp.sum(weights, axis=1, keepdims=True), (SUB * rows, 128))
            mixed = jnp.dot(weights.astype(jnp.bfloat16), kv_ref[:, :latent], preferred_element_type=jnp.float32)
            if not first_call:
                total = total + factor * total_in[span(base), :]
                mixed = mixed + widen(factor, latent // 128) * sum_in[span(base), :]
            if last_call:
                mixed = mixed * widen(1.0 / total, latent // 128)
                mixed_ref[span(base), :] = mixed.astype(jnp.bfloat16)
            else:
                sum_out[span(base), :] = mixed
                most_out[span(base), :] = most
                total_out[span(base), :] = total
            now = later
        return carry

    lax.fori_loop(0, heads // SPAN, group, 0)
    if last_call:
        value_heads(mixed_ref, vu_ref, out_ref)


def params(limit=24):
    return pltpu.CompilerParams(vmem_limit_bytes=limit * 2**20)


def shards(latent_raw, kv_gain, query_nope, query_rope, key_up, value_up, doc_lengths):
    rows = query_nope.shape[0]
    heads, nope, latent = key_up.shape
    value = value_up.shape[2]
    half_rows, full = latent_raw.shape
    rope = full - latent
    wide = latent + 128
    ctx_size = lax.axis_size("ctx")
    scale = (nope + rope) ** (-0.5)

    def plane_shift(array, planes):
        steps = planes * PLANE
        return lax.ppermute(array, "ctx", [(s, (s + steps) % ctx_size) for s in range(ctx_size)])

    def swap_ctx(array, bit):
        return lax.ppermute(array, "ctx", [(s, s ^ bit) for s in range(ctx_size)])

    def swap_head(array):
        return lax.ppermute(array, "head", [(0, 1), (1, 0)])

    one = plane_shift(latent_raw, 1)
    two = plane_shift(latent_raw, 2)
    table = jax.ShapeDtypeStruct((3, half_rows, 128), jnp.float32)
    queries, cos, sin = pl.pallas_call(
        query_kernel,
        out_shape=(jax.ShapeDtypeStruct((heads * rows, wide), jnp.bfloat16), table, table),
        in_specs=[HBM] * 4,
        out_specs=[VMEM] * 3,
        scratch_shapes=[
            pltpu.VMEM(query_nope.shape, jnp.bfloat16),
            pltpu.VMEM(query_rope.shape, jnp.bfloat16),
            pltpu.VMEM(key_up.shape, jnp.bfloat16),
            pltpu.SMEM(doc_lengths.shape, jnp.int32),
            pltpu.SemaphoreType.DMA((heads // GROUP + 1, 2)),
        ],
        compiler_params=params(),
        cost_estimate=pl.CostEstimate(
            flops=2 * heads * rows * nope * latent, bytes_accessed=8 * 2**20, transcendentals=0
        ),
        name="queries",
    )(
        *(pltpu.with_memory_space_constraint(array, pltpu.HBM) for array in (doc_lengths, query_nope, query_rope, key_up))
    )
    near, send = pl.pallas_call(
        rows_kernel,
        out_shape=(
            jax.ShapeDtypeStruct((3, half_rows, full), jnp.bfloat16),
            jax.ShapeDtypeStruct((2, half_rows, full), jnp.bfloat16),
        ),
        in_specs=[VMEM] * 6,
        out_specs=[VMEM] * 2,
        compiler_params=params(),
        name="rows",
    )(latent_raw, one, two, kv_gain[None], cos, sin)
    across = swap_ctx(send, 2)
    side = swap_head(near)
    near_pieces = [(near, (False, False, False)), (swap_ctx(near, 1), (False, True, False))]

    state_shape = (
        jax.ShapeDtypeStruct((heads * rows, latent), jnp.float32),
        jax.ShapeDtypeStruct((heads * rows, 128), jnp.float32),
        jax.ShapeDtypeStruct((heads * rows, 128), jnp.float32),
    )
    names = iter(("attend_near", "attend_far"))

    def attend(part, state, last=False):
        pieces, layout = zip(*part)
        keys = 2 * half_rows * len(pieces)
        scratch = [pltpu.VMEM((keys, wide), jnp.bfloat16)]
        if last:
            scratch = [pltpu.VMEM((heads * rows, latent), jnp.bfloat16)] + scratch
        extra = (value_up,) if last else ()
        return pl.pallas_call(
            functools.partial(attend_kernel, layout, scale, not state, last),
            out_shape=jax.ShapeDtypeStruct((rows, heads * value), jnp.bfloat16) if last else state_shape,
            in_specs=[SMEM] + [VMEM] * (1 + len(pieces) + len(state) + len(extra)),
            out_specs=VMEM if last else [VMEM] * 3,
            scratch_shapes=scratch,
            compiler_params=params(),
            name=next(names),
        )(doc_lengths, queries, *pieces, *state, *extra)

    corner = swap_head(across)
    across_pieces = [(across, (True, False, False)), (swap_ctx(across, 1), (True, True, False))]
    state = attend(near_pieces + across_pieces, ())
    side, corner, *state = lax.optimization_barrier((side, corner, *state))
    side_pieces = [(side, (False, False, True)), (swap_ctx(side, 1), (False, True, True))]
    corner_pieces = [(corner, (True, False, True)), (swap_ctx(corner, 1), (True, True, True))]
    return attend(side_pieces + corner_pieces, state, last=True)


def solution(mesh):
    return jax.shard_map(
        shards,
        mesh=mesh,
        in_specs=(
            P(("ctx", "head"), None),
            P(),
            P("ctx", "head"),
            P("ctx", "head"),
            P("head", None, None),
            P("head", None, None),
            P(),
        ),
        out_specs=P("ctx", "head"),
        check_vma=False,
    )
```

```python
import functools
import math

import jax
import jax.numpy as jnp
import numpy as np
from jax import lax
from jax.experimental import pallas as pl
from jax.experimental.pallas import tpu as pltpu
from jax.sharding import PartitionSpec as P

epsilon = 1e-06
masked_score = -1e30
PLANE = 4
GROUP = 8
SUB = 4
VALUE_GROUP = 8
HBM = pl.BlockSpec(memory_space=pltpu.HBM)
VMEM = pl.BlockSpec(memory_space=pltpu.VMEM)
SMEM = pl.BlockSpec(memory_space=pltpu.SMEM)


def begin_of(positions, lengths_ref):
    begin = jnp.zeros_like(positions)
    start = jnp.int32(0)
    for doc in range(lengths_ref.shape[0] - 1):
        start = start + lengths_ref[doc]
        begin = jnp.where(positions >= start, start, begin)
    return begin


def half_start(plane, flip_y, flip_core, flip_head, block_rows, half_rows):
    ctx = lax.axis_index("ctx")
    head = lax.axis_index("head")
    core = lax.rem(ctx, 2)
    row = lax.rem(ctx // 2, 2)
    base = ctx // PLANE - plane
    row = 1 - row if flip_y else row
    core = 1 - core if flip_core else core
    head = 1 - head if flip_head else head
    return (base * PLANE + row * 2 + core) * block_rows + head * half_rows


def frequencies(rope, shape):
    half = rope // 2
    exponents = np.float32(-2.0) * np.arange(half, dtype=np.float32) / np.float32(rope)
    values = np.float32(10000.0) ** exponents
    lane = lax.rem(lax.broadcasted_iota(jnp.int32, shape, 1), half)
    freq = jnp.zeros(shape, jnp.float32)
    for index in range(half):
        freq = jnp.where(lane == index, float(values[index]), freq)
    return freq


def query_kernel(lengths_hbm, qn_hbm, qr_hbm, ku_hbm, q_ref, cos_ref, sin_ref, qn_ref, qr_ref, ku_ref, lengths_ref, sems):
    rows = qn_ref.shape[0]
    heads, nope, latent = ku_ref.shape
    rope = qr_ref.shape[1] // heads
    groups = heads // GROUP

    def copies(index):
        head = index * GROUP
        cols = pl.ds(head * nope, GROUP * nope)
        part = pl.ds(head, GROUP)
        return [
            pltpu.make_async_copy(qn_hbm.at[:, cols], qn_ref.at[:, cols], sems.at[index, 0]),
            pltpu.make_async_copy(ku_hbm.at[part], ku_ref.at[part], sems.at[index, 1]),
        ]

    rope_copy = pltpu.make_async_copy(qr_hbm, qr_ref, sems.at[groups, 0])
    lengths_copy = pltpu.make_async_copy(lengths_hbm, lengths_ref, sems.at[groups, 1])
    lengths_copy.start()
    rope_copy.start()
    for index in range(groups):
        for copy in copies(index):
            copy.start()
    lengths_copy.wait()
    ctx = lax.axis_index("ctx")
    freq = frequencies(rope, (8, 128))[0:1, :]
    key_rows = rows // 2
    for plane in range(3):
        first = half_start(plane, False, False, False, rows, key_rows)
        pos = first + lax.broadcasted_iota(jnp.int32, (key_rows, 128), 0)
        angle = (pos - begin_of(pos, lengths_ref)).astype(jnp.float32) * freq
        cos_ref[plane] = jnp.cos(angle)
        sin_ref[plane] = jnp.sin(angle)
    pos = ctx * rows + lax.broadcasted_iota(jnp.int32, (rows, 128), 0)
    angle = (pos - begin_of(pos, lengths_ref)).astype(jnp.float32) * freq
    lane = lax.broadcasted_iota(jnp.int32, (rows, 128), 1)
    low = lax.rem(lane, rope) < rope // 2
    cos = jnp.cos(angle)
    sin = jnp.sin(angle)
    sin = jnp.where(low, -sin, sin)
    rope_copy.wait()
    for index in range(groups):
        for copy in copies(index):
            copy.wait()
        for head in range(index * GROUP, (index + 1) * GROUP, 2):
            pair = qr_ref[:, head * rope : (head + 2) * rope].astype(jnp.float32)
            partner = jnp.where(low, pltpu.roll(pair, 128 - rope // 2, 1), pltpu.roll(pair, rope // 2, 1))
            rotated = pair * cos + partner * sin
            for k, part in enumerate((rotated, pltpu.roll(rotated, rope, 1))):
                at = slice((head + k) * rows, (head + k + 1) * rows)
                nope_rows = qn_ref[:, (head + k) * nope : (head + k + 1) * nope]
                absorbed = jnp.dot(nope_rows, ku_ref[head + k], preferred_element_type=jnp.float32)
                q_ref[at, :latent] = absorbed.astype(jnp.bfloat16)
                q_ref[at, latent:] = jnp.where(lane < rope, part, 0.0).astype(jnp.bfloat16)


def rows_kernel(own_ref, one_ref, two_ref, gain_ref, cos_ref, sin_ref, rows_ref, send_ref):
    latent = gain_ref.shape[1]
    full = own_ref.shape[1]
    half = (full - latent) // 2
    row = lax.rem(lax.axis_index("ctx") // 2, 2)
    gain = gain_ref[0:1, :]
    for plane, raw_ref in enumerate((own_ref, one_ref, two_ref)):
        part = raw_ref[:, :latent].astype(jnp.float32)
        mean = jnp.mean(part * part, axis=1, keepdims=True)
        normed = part * lax.rsqrt(mean + epsilon) * gain
        rope = raw_ref[:, latent:].astype(jnp.float32)
        first, second = rope[:, :half], rope[:, half:]
        cos, sin = cos_ref[plane][:, :half], sin_ref[plane][:, :half]
        turned = jnp.concatenate([first * cos - second * sin, second * cos + first * sin], axis=1)
        rows_ref[plane, :, :latent] = normed.astype(jnp.bfloat16)
        rows_ref[plane, :, latent:] = turned.astype(jnp.bfloat16)
    send_ref[...] = rows_ref[pl.ds(row, 2)]


def widen(column, count):
    return jnp.concatenate([column] * count, axis=1)


def value_heads(mixed_ref, vu_ref, held_ref, out_ref, sems):
    heads, latent, value = vu_ref.shape
    rows = held_ref.shape[0]
    copies = []
    for head in range(heads):
        cols = slice(head * value, (head + 1) * value)
        result = jnp.dot(
            mixed_ref[head * rows : (head + 1) * rows, :], vu_ref[head], preferred_element_type=jnp.float32
        )
        held_ref[:, cols] = result.astype(jnp.bfloat16)
        if (head + 1) % VALUE_GROUP == 0:
            group = head // VALUE_GROUP
            cols = slice(group * VALUE_GROUP * value, (head + 1) * value)
            copies.append(pltpu.make_async_copy(held_ref.at[:, cols], out_ref.at[:, cols], sems.at[group]))
            copies[-1].start()
    for copy in copies:
        copy.wait()


def attend_kernel(layout, scale, first_call, last_call, lengths_ref, q_ref, *refs):
    count = len(layout)
    piece_refs, refs = refs[:count], refs[count:]
    if not first_call:
        sum_in, most_in, total_in = refs[:3]
        refs = refs[3:]
    if last_call:
        vu_ref, out_ref, mixed_ref, held_ref, sems, kv_ref = refs
        latent = mixed_ref.shape[1]
    else:
        sum_out, most_out, total_out, kv_ref = refs
        latent = sum_out.shape[1]
    half_rows = piece_refs[0].shape[1]
    rows = 2 * half_rows
    heads = q_ref.shape[0] // rows
    ctx = lax.axis_index("ctx")
    core = lax.rem(ctx, 2)
    row = lax.rem(ctx // 2, 2)
    keys = kv_ref.shape[0]
    full = piece_refs[0].shape[2]
    kv_ref[:, full:] = jnp.zeros((keys, kv_ref.shape[1] - full), jnp.bfloat16)
    firsts = []
    for step in range(2):
        for (flip_y, flip_core, flip_head), ref in zip(layout, piece_refs):
            if flip_y:
                index, plane = 0, 1 - row
            else:
                index = plane = 1 - core if flip_core else 0
            at = len(firsts) * half_rows
            kv_ref[at : at + half_rows, :full] = ref[index + step]
            firsts.append(half_start(plane + step, flip_y, flip_core, flip_head, rows, half_rows))
    earliest = begin_of(ctx * rows, lengths_ref)
    older_live = functools.reduce(jnp.maximum, firsts[count:]) + half_rows > earliest
    exponent = scale * math.log2(math.e)

    def span(base):
        return slice(base * rows, (base + SUB) * rows)

    def visit(pieces):
        width = pieces * half_rows
        lane = lax.broadcasted_iota(jnp.int32, (rows, width), 1)
        key_pos = lane + firsts[0]
        for piece in range(1, pieces):
            at = piece * half_rows
            key_pos = jnp.where(lane >= at, lane + (firsts[piece] - at), key_pos)
        pos = ctx * rows + lax.broadcasted_iota(jnp.int32, (rows, width), 0)
        live = (key_pos <= pos) & (key_pos >= begin_of(pos, lengths_ref))

        def scores(base):
            return lax.dot_general(
                q_ref[span(base), :], kv_ref[:width, :], (((1,), (1,)), ((), ())), preferred_element_type=jnp.float32
            )

        def finish(base, weights, total, most, factor):
            mixed = jnp.dot(weights, kv_ref[:width, :latent], preferred_element_type=jnp.float32)
            if not first_call:
                total = total + factor * total_in[span(base), :]
                mixed = mixed + widen(factor, latent // 128) * sum_in[span(base), :]
            if last_call:
                mixed = mixed * widen(1.0 / total, latent // 128)
                mixed_ref[span(base), :] = mixed.astype(jnp.bfloat16)
            else:
                sum_out[span(base), :] = mixed
                most_out[span(base), :] = most
                total_out[span(base), :] = total

        now = scores(0)
        waiting = None
        for base in range(0, heads, SUB):
            later = scores(base + SUB) if base + SUB < heads else None
            now = jnp.where(live[None], now.reshape(SUB, rows, width), masked_score).reshape(SUB * rows, width)
            most = jnp.broadcast_to(jnp.max(now, axis=1, keepdims=True), (SUB * rows, 128))
            factor = None
            if not first_call:
                before = most_in[span(base), :]
                most = jnp.maximum(most, before)
                factor = jnp.exp2((before - most) * exponent)
            weights = jnp.exp2((now - widen(most, width // 128)) * exponent)
            total = jnp.broadcast_to(jnp.sum(weights, axis=1, keepdims=True), (SUB * rows, 128))
            if waiting:
                finish(*waiting)
            waiting = (base, weights.astype(jnp.bfloat16), total, most, factor)
            now = later
        finish(*waiting)

    @pl.when(older_live)
    def all_pieces():
        visit(2 * count)

    @pl.when(jnp.logical_not(older_live))
    def newer_pieces():
        visit(count)

    if last_call:
        value_heads(mixed_ref, vu_ref, held_ref, out_ref, sems)


def params(limit=24):
    return pltpu.CompilerParams(vmem_limit_bytes=limit * 2**20)


def shards(latent_raw, kv_gain, query_nope, query_rope, key_up, value_up, doc_lengths):
    rows = query_nope.shape[0]
    heads, nope, latent = key_up.shape
    value = value_up.shape[2]
    half_rows, full = latent_raw.shape
    rope = full - latent
    wide = latent + 128
    ctx_size = lax.axis_size("ctx")
    scale = (nope + rope) ** (-0.5)

    def plane_shift(array, planes):
        steps = planes * PLANE
        return lax.ppermute(array, "ctx", [(s, (s + steps) % ctx_size) for s in range(ctx_size)])

    def swap_ctx(array, bit):
        return lax.ppermute(array, "ctx", [(s, s ^ bit) for s in range(ctx_size)])

    def swap_head(array):
        return lax.ppermute(array, "head", [(0, 1), (1, 0)])

    one = plane_shift(latent_raw, 1)
    two = plane_shift(latent_raw, 2)
    table = jax.ShapeDtypeStruct((3, half_rows, 128), jnp.float32)
    queries, cos, sin = pl.pallas_call(
        query_kernel,
        out_shape=(jax.ShapeDtypeStruct((heads * rows, wide), jnp.bfloat16), table, table),
        in_specs=[HBM] * 4,
        out_specs=[VMEM] * 3,
        scratch_shapes=[
            pltpu.VMEM(query_nope.shape, jnp.bfloat16),
            pltpu.VMEM(query_rope.shape, jnp.bfloat16),
            pltpu.VMEM(key_up.shape, jnp.bfloat16),
            pltpu.SMEM(doc_lengths.shape, jnp.int32),
            pltpu.SemaphoreType.DMA((heads // GROUP + 1, 2)),
        ],
        compiler_params=params(),
        cost_estimate=pl.CostEstimate(
            flops=2 * heads * rows * nope * latent, bytes_accessed=8 * 2**20, transcendentals=0
        ),
        name="queries",
    )(
        *(pltpu.with_memory_space_constraint(array, pltpu.HBM) for array in (doc_lengths, query_nope, query_rope, key_up))
    )
    near, send = pl.pallas_call(
        rows_kernel,
        out_shape=(
            jax.ShapeDtypeStruct((3, half_rows, full), jnp.bfloat16),
            jax.ShapeDtypeStruct((2, half_rows, full), jnp.bfloat16),
        ),
        in_specs=[VMEM] * 6,
        out_specs=[VMEM] * 2,
        compiler_params=params(),
        name="rows",
    )(latent_raw, one, two, kv_gain[None], cos, sin)
    across = swap_ctx(send, 2)
    side = swap_head(near)
    near_pieces = [(near, (False, False, False)), (swap_ctx(near, 1), (False, True, False))]

    state_shape = (
        jax.ShapeDtypeStruct((heads * rows, latent), jnp.float32),
        jax.ShapeDtypeStruct((heads * rows, 128), jnp.float32),
        jax.ShapeDtypeStruct((heads * rows, 128), jnp.float32),
    )
    names = iter(("attend_near", "attend_far"))

    def attend(part, state, last=False):
        pieces, layout = zip(*part)
        keys = 2 * half_rows * len(pieces)
        scratch = [pltpu.VMEM((keys, wide), jnp.bfloat16)]
        if last:
            scratch = [
                pltpu.VMEM((heads * rows, latent), jnp.bfloat16),
                pltpu.VMEM((rows, heads * value), jnp.bfloat16),
                pltpu.SemaphoreType.DMA((heads // VALUE_GROUP,)),
            ] + scratch
        extra = (value_up,) if last else ()
        return pl.pallas_call(
            functools.partial(attend_kernel, layout, scale, not state, last),
            out_shape=jax.ShapeDtypeStruct((rows, heads * value), jnp.bfloat16) if last else state_shape,
            in_specs=[SMEM] + [VMEM] * (1 + len(pieces) + len(state) + len(extra)),
            out_specs=HBM if last else [VMEM] * 3,
            scratch_shapes=scratch,
            compiler_params=params(),
            name=next(names),
        )(doc_lengths, queries, *pieces, *state, *extra)

    corner = swap_head(across)
    across_pieces = [(across, (True, False, False)), (swap_ctx(across, 1), (True, True, False))]
    state = attend(near_pieces + across_pieces, ())
    side, corner, *state = lax.optimization_barrier((side, corner, *state))
    side_pieces = [(side, (False, False, True)), (swap_ctx(side, 1), (False, True, True))]
    corner_pieces = [(corner, (True, False, True)), (swap_ctx(corner, 1), (True, True, True))]
    return attend(side_pieces + corner_pieces, state, last=True)


def solution(mesh):
    return jax.shard_map(
        shards,
        mesh=mesh,
        in_specs=(
            P(("ctx", "head"), None),
            P(),
            P("ctx", "head"),
            P("ctx", "head"),
            P("head", None, None),
            P("head", None, None),
            P(),
        ),
        out_specs=P("ctx", "head"),
        check_vma=False,
    )
```

```python
import functools
import math

import jax
import jax.numpy as jnp
import numpy as np
from jax import lax
from jax.experimental import pallas as pl
from jax.experimental.pallas import tpu as pltpu
from jax.sharding import PartitionSpec as P

epsilon = 1e-06
masked_score = -1e30
PLANE = 4
GROUP = 8
SUB = 4
VALUE_GROUP = 8
HBM = pl.BlockSpec(memory_space=pltpu.HBM)
VMEM = pl.BlockSpec(memory_space=pltpu.VMEM)
SMEM = pl.BlockSpec(memory_space=pltpu.SMEM)


def begin_of(positions, lengths_ref):
    begin = jnp.zeros_like(positions)
    start = jnp.int32(0)
    for doc in range(lengths_ref.shape[0] - 1):
        start = start + lengths_ref[doc]
        begin = jnp.where(positions >= start, start, begin)
    return begin


def half_start(plane, flip_y, flip_core, flip_head, block_rows, half_rows):
    ctx = lax.axis_index("ctx")
    head = lax.axis_index("head")
    core = lax.rem(ctx, 2)
    row = lax.rem(ctx // 2, 2)
    base = ctx // PLANE - plane
    row = 1 - row if flip_y else row
    core = 1 - core if flip_core else core
    head = 1 - head if flip_head else head
    return (base * PLANE + row * 2 + core) * block_rows + head * half_rows


def frequencies(rope, shape):
    half = rope // 2
    exponents = np.float32(-2.0) * np.arange(half, dtype=np.float32) / np.float32(rope)
    values = np.float32(10000.0) ** exponents
    lane = lax.rem(lax.broadcasted_iota(jnp.int32, shape, 1), half)
    freq = jnp.zeros(shape, jnp.float32)
    for index in range(half):
        freq = jnp.where(lane == index, float(values[index]), freq)
    return freq


def query_kernel(lengths_hbm, qn_hbm, qr_hbm, ku_hbm, q_ref, cos_ref, sin_ref, qn_ref, qr_ref, ku_ref, lengths_ref, sems):
    rows = qn_ref.shape[0]
    heads, nope, latent = ku_ref.shape
    rope = qr_ref.shape[1] // heads
    groups = heads // GROUP

    def copies(index):
        head = index * GROUP
        cols = pl.ds(head * nope, GROUP * nope)
        part = pl.ds(head, GROUP)
        return [
            pltpu.make_async_copy(qn_hbm.at[:, cols], qn_ref.at[:, cols], sems.at[index, 0]),
            pltpu.make_async_copy(ku_hbm.at[part], ku_ref.at[part], sems.at[index, 1]),
        ]

    rope_copy = pltpu.make_async_copy(qr_hbm, qr_ref, sems.at[groups, 0])
    lengths_copy = pltpu.make_async_copy(lengths_hbm, lengths_ref, sems.at[groups, 1])
    lengths_copy.start()
    rope_copy.start()
    for index in range(groups):
        for copy in copies(index):
            copy.start()
    lengths_copy.wait()
    ctx = lax.axis_index("ctx")
    freq = frequencies(rope, (8, 128))[0:1, :]
    key_rows = rows // 2
    for plane in range(3):
        first = half_start(plane, False, False, False, rows, key_rows)
        pos = first + lax.broadcasted_iota(jnp.int32, (key_rows, 128), 0)
        angle = (pos - begin_of(pos, lengths_ref)).astype(jnp.float32) * freq
        cos_ref[plane] = jnp.cos(angle)
        sin_ref[plane] = jnp.sin(angle)
    pos = ctx * rows + lax.broadcasted_iota(jnp.int32, (rows, 128), 0)
    angle = (pos - begin_of(pos, lengths_ref)).astype(jnp.float32) * freq
    lane = lax.broadcasted_iota(jnp.int32, (rows, 128), 1)
    low = lax.rem(lane, rope) < rope // 2
    cos = jnp.cos(angle)
    sin = jnp.sin(angle)
    sin = jnp.where(low, -sin, sin)
    rope_copy.wait()
    for index in range(groups):
        for copy in copies(index):
            copy.wait()
        for head in range(index * GROUP, (index + 1) * GROUP, 2):
            pair = qr_ref[:, head * rope : (head + 2) * rope].astype(jnp.float32)
            partner = jnp.where(low, pltpu.roll(pair, 128 - rope // 2, 1), pltpu.roll(pair, rope // 2, 1))
            rotated = pair * cos + partner * sin
            for k, part in enumerate((rotated, pltpu.roll(rotated, rope, 1))):
                at = slice((head + k) * rows, (head + k + 1) * rows)
                nope_rows = qn_ref[:, (head + k) * nope : (head + k + 1) * nope]
                absorbed = jnp.dot(nope_rows, ku_ref[head + k], preferred_element_type=jnp.float32)
                q_ref[at, :latent] = absorbed.astype(jnp.bfloat16)
                q_ref[at, latent:] = jnp.where(lane < rope, part, 0.0).astype(jnp.bfloat16)


def rows_kernel(own_ref, one_ref, two_ref, gain_ref, cos_ref, sin_ref, rows_ref, send_ref):
    latent = gain_ref.shape[1]
    full = own_ref.shape[1]
    half = (full - latent) // 2
    row = lax.rem(lax.axis_index("ctx") // 2, 2)
    gain = gain_ref[0:1, :]
    for plane, raw_ref in enumerate((own_ref, one_ref, two_ref)):
        part = raw_ref[:, :latent].astype(jnp.float32)
        mean = jnp.mean(part * part, axis=1, keepdims=True)
        normed = part * lax.rsqrt(mean + epsilon) * gain
        rope = raw_ref[:, latent:].astype(jnp.float32)
        first, second = rope[:, :half], rope[:, half:]
        cos, sin = cos_ref[plane][:, :half], sin_ref[plane][:, :half]
        turned = jnp.concatenate([first * cos - second * sin, second * cos + first * sin], axis=1)
        rows_ref[plane, :, :latent] = normed.astype(jnp.bfloat16)
        rows_ref[plane, :, latent:] = turned.astype(jnp.bfloat16)
    send_ref[...] = rows_ref[pl.ds(row, 2)]


def widen(column, count):
    return jnp.concatenate([column] * count, axis=1)


def value_heads(mixed_ref, vu_ref, held_ref, out_ref, sems):
    heads, latent, value = vu_ref.shape
    rows = held_ref.shape[0]
    copies = []
    for head in range(heads):
        cols = slice(head * value, (head + 1) * value)
        result = jnp.dot(
            mixed_ref[head * rows : (head + 1) * rows, :], vu_ref[head], preferred_element_type=jnp.float32
        )
        held_ref[:, cols] = result.astype(jnp.bfloat16)
        if (head + 1) % VALUE_GROUP == 0:
            group = head // VALUE_GROUP
            cols = slice(group * VALUE_GROUP * value, (head + 1) * value)
            copies.append(pltpu.make_async_copy(held_ref.at[:, cols], out_ref.at[:, cols], sems.at[group]))
            copies[-1].start()
    for copy in copies:
        copy.wait()


def attend_kernel(layout, scale, first_call, last_call, lengths_ref, q_ref, *refs):
    count = len(layout)
    piece_refs, refs = refs[:count], refs[count:]
    if not first_call:
        sum_in, most_in, total_in = refs[:3]
        refs = refs[3:]
    if last_call:
        vu_ref, out_ref, mixed_ref, held_ref, sems, kv_ref = refs
        latent = mixed_ref.shape[1]
    else:
        sum_out, most_out, total_out, kv_ref = refs
        latent = sum_out.shape[1]
    half_rows = piece_refs[0].shape[1]
    rows = 2 * half_rows
    heads = q_ref.shape[0] // rows
    ctx = lax.axis_index("ctx")
    core = lax.rem(ctx, 2)
    row = lax.rem(ctx // 2, 2)
    keys = kv_ref.shape[0]
    full = piece_refs[0].shape[2]
    kv_ref[:, full:] = jnp.zeros((keys, kv_ref.shape[1] - full), jnp.bfloat16)
    firsts = []
    for step in range(2):
        for (flip_y, flip_core, flip_head), ref in zip(layout, piece_refs):
            if flip_y:
                index, plane = 0, 1 - row
            else:
                index = plane = 1 - core if flip_core else 0
            at = len(firsts) * half_rows
            kv_ref[at : at + half_rows, :full] = ref[index + step]
            firsts.append(half_start(plane + step, flip_y, flip_core, flip_head, rows, half_rows))
    earliest = begin_of(ctx * rows, lengths_ref)
    older_live = functools.reduce(jnp.maximum, firsts[count:]) + half_rows > earliest
    exponent = scale * math.log2(math.e)

    def span(base):
        return slice(base * rows, (base + SUB) * rows)

    def visit(pieces):
        width = pieces * half_rows
        lane = lax.broadcasted_iota(jnp.int32, (rows, width), 1)
        key_pos = lane + firsts[0]
        for piece in range(1, pieces):
            at = piece * half_rows
            key_pos = jnp.where(lane >= at, lane + (firsts[piece] - at), key_pos)
        pos = ctx * rows + lax.broadcasted_iota(jnp.int32, (rows, width), 0)
        live = (key_pos <= pos) & (key_pos >= begin_of(pos, lengths_ref))

        def scores(base):
            return lax.dot_general(
                q_ref[span(base), :], kv_ref[:width, :], (((1,), (1,)), ((), ())), preferred_element_type=jnp.float32
            )

        def finish(base, weights, total, most, factor):
            mixed = jnp.dot(weights, kv_ref[:width, :latent], preferred_element_type=jnp.float32)
            if not first_call:
                total = total + factor * total_in[span(base), :]
                mixed = mixed + widen(factor, latent // 128) * sum_in[span(base), :]
            if last_call:
                mixed = mixed * widen(1.0 / total, latent // 128)
                mixed_ref[span(base), :] = mixed.astype(jnp.bfloat16)
            else:
                sum_out[span(base), :] = mixed
                most_out[span(base), :] = most
                total_out[span(base), :] = total

        now = scores(0)
        waiting = None
        for base in range(0, heads, SUB):
            later = scores(base + SUB) if base + SUB < heads else None
            now = jnp.where(live[None], now.reshape(SUB, rows, width), masked_score).reshape(SUB * rows, width)
            most = jnp.broadcast_to(jnp.max(now, axis=1, keepdims=True), (SUB * rows, 128))
            factor = None
            if not first_call:
                before = most_in[span(base), :]
                most = jnp.maximum(most, before)
                factor = jnp.exp2((before - most) * exponent)
            weights = jnp.exp2((now - widen(most, width // 128)) * exponent)
            total = jnp.broadcast_to(jnp.sum(weights, axis=1, keepdims=True), (SUB * rows, 128))
            if waiting:
                finish(*waiting)
            waiting = (base, weights.astype(jnp.bfloat16), total, most, factor)
            now = later
        finish(*waiting)

    @pl.when(older_live)
    def all_pieces():
        visit(2 * count)

    @pl.when(jnp.logical_not(older_live))
    def newer_pieces():
        visit(count)

    if last_call:
        value_heads(mixed_ref, vu_ref, held_ref, out_ref, sems)


def params(limit=24):
    return pltpu.CompilerParams(vmem_limit_bytes=limit * 2**20)


def shards(latent_raw, kv_gain, query_nope, query_rope, key_up, value_up, doc_lengths):
    rows = query_nope.shape[0]
    heads, nope, latent = key_up.shape
    value = value_up.shape[2]
    half_rows, full = latent_raw.shape
    rope = full - latent
    wide = latent + 128
    ctx_size = lax.axis_size("ctx")
    scale = (nope + rope) ** (-0.5)

    def plane_shift(array, planes):
        steps = planes * PLANE
        return lax.ppermute(array, "ctx", [(s, (s + steps) % ctx_size) for s in range(ctx_size)])

    def swap_ctx(array, bit):
        return lax.ppermute(array, "ctx", [(s, s ^ bit) for s in range(ctx_size)])

    def swap_head(array):
        return lax.ppermute(array, "head", [(0, 1), (1, 0)])

    one = plane_shift(latent_raw, 1)
    two = plane_shift(latent_raw, 2)
    table = jax.ShapeDtypeStruct((3, half_rows, 128), jnp.float32)
    queries, cos, sin = pl.pallas_call(
        query_kernel,
        out_shape=(jax.ShapeDtypeStruct((heads * rows, wide), jnp.bfloat16), table, table),
        in_specs=[HBM] * 4,
        out_specs=[VMEM] * 3,
        scratch_shapes=[
            pltpu.VMEM(query_nope.shape, jnp.bfloat16),
            pltpu.VMEM(query_rope.shape, jnp.bfloat16),
            pltpu.VMEM(key_up.shape, jnp.bfloat16),
            pltpu.SMEM(doc_lengths.shape, jnp.int32),
            pltpu.SemaphoreType.DMA((heads // GROUP + 1, 2)),
        ],
        compiler_params=params(),
        cost_estimate=pl.CostEstimate(
            flops=2 * heads * rows * nope * latent, bytes_accessed=8 * 2**20, transcendentals=0
        ),
        name="queries",
    )(
        *(pltpu.with_memory_space_constraint(array, pltpu.HBM) for array in (doc_lengths, query_nope, query_rope, key_up))
    )
    near, send = pl.pallas_call(
        rows_kernel,
        out_shape=(
            jax.ShapeDtypeStruct((3, half_rows, full), jnp.bfloat16),
            jax.ShapeDtypeStruct((2, half_rows, full), jnp.bfloat16),
        ),
        in_specs=[VMEM] * 6,
        out_specs=[VMEM] * 2,
        compiler_params=params(),
        name="rows",
    )(latent_raw, one, two, kv_gain[None], cos, sin)
    across = swap_ctx(send, 2)
    side = swap_head(near)
    near_pieces = [(near, (False, False, False)), (swap_ctx(near, 1), (False, True, False))]

    state_shape = (
        jax.ShapeDtypeStruct((heads * rows, latent), jnp.float32),
        jax.ShapeDtypeStruct((heads * rows, 128), jnp.float32),
        jax.ShapeDtypeStruct((heads * rows, 128), jnp.float32),
    )
    names = iter(("attend_near", "attend_across", "attend_far"))

    def attend(part, state, last=False):
        pieces, layout = zip(*part)
        keys = 2 * half_rows * len(pieces)
        scratch = [pltpu.VMEM((keys, wide), jnp.bfloat16)]
        if last:
            scratch = [
                pltpu.VMEM((heads * rows, latent), jnp.bfloat16),
                pltpu.VMEM((rows, heads * value), jnp.bfloat16),
                pltpu.SemaphoreType.DMA((heads // VALUE_GROUP,)),
            ] + scratch
        extra = (value_up,) if last else ()
        return pl.pallas_call(
            functools.partial(attend_kernel, layout, scale, not state, last),
            out_shape=jax.ShapeDtypeStruct((rows, heads * value), jnp.bfloat16) if last else state_shape,
            in_specs=[SMEM] + [VMEM] * (1 + len(pieces) + len(state) + len(extra)),
            out_specs=HBM if last else [VMEM] * 3,
            scratch_shapes=scratch,
            compiler_params=params(18 if last else 8),
            name=next(names),
        )(doc_lengths, queries, *pieces, *state, *extra)

    state = attend(near_pieces, ())
    across, *state = lax.optimization_barrier((across, *state))
    corner = swap_head(across)
    across_pieces = [(across, (True, False, False)), (swap_ctx(across, 1), (True, True, False))]
    state = attend(across_pieces, state)
    side, corner, *state = lax.optimization_barrier((side, corner, *state))
    side_pieces = [(side, (False, False, True)), (swap_ctx(side, 1), (False, True, True))]
    corner_pieces = [(corner, (True, False, True)), (swap_ctx(corner, 1), (True, True, True))]
    return attend(side_pieces + corner_pieces, state, last=True)


def solution(mesh):
    return jax.shard_map(
        shards,
        mesh=mesh,
        in_specs=(
            P(("ctx", "head"), None),
            P(),
            P("ctx", "head"),
            P("ctx", "head"),
            P("head", None, None),
            P("head", None, None),
            P(),
        ),
        out_specs=P("ctx", "head"),
        check_vma=False,
    )
```

```python
import functools
import math

import jax
import jax.numpy as jnp
import numpy as np
from jax import lax
from jax.experimental import pallas as pl
from jax.experimental.pallas import tpu as pltpu
from jax.sharding import PartitionSpec as P

epsilon = 1e-06
masked_score = -1e30
PLANE = 4
GROUP = 8
SUB = 4
VALUE_GROUP = 8
HBM = pl.BlockSpec(memory_space=pltpu.HBM)
VMEM = pl.BlockSpec(memory_space=pltpu.VMEM)
SMEM = pl.BlockSpec(memory_space=pltpu.SMEM)


def begin_of(positions, lengths_ref):
    begin = jnp.zeros_like(positions)
    start = jnp.int32(0)
    for doc in range(lengths_ref.shape[0] - 1):
        start = start + lengths_ref[doc]
        begin = jnp.where(positions >= start, start, begin)
    return begin


def half_start(plane, flip_y, flip_core, flip_head, block_rows, half_rows):
    ctx = lax.axis_index("ctx")
    head = lax.axis_index("head")
    core = lax.rem(ctx, 2)
    row = lax.rem(ctx // 2, 2)
    base = ctx // PLANE - plane
    row = 1 - row if flip_y else row
    core = 1 - core if flip_core else core
    head = 1 - head if flip_head else head
    return (base * PLANE + row * 2 + core) * block_rows + head * half_rows


def frequencies(rope, shape):
    half = rope // 2
    exponents = np.float32(-2.0) * np.arange(half, dtype=np.float32) / np.float32(rope)
    values = np.float32(10000.0) ** exponents
    lane = lax.rem(lax.broadcasted_iota(jnp.int32, shape, 1), half)
    freq = jnp.zeros(shape, jnp.float32)
    for index in range(half):
        freq = jnp.where(lane == index, float(values[index]), freq)
    return freq


def query_kernel(lengths_hbm, qn_hbm, qr_hbm, ku_hbm, q_ref, cos_ref, sin_ref, qn_ref, qr_ref, ku_ref, lengths_ref, sems):
    rows = qn_ref.shape[0]
    heads, nope, latent = ku_ref.shape
    rope = qr_ref.shape[1] // heads
    groups = heads // GROUP

    def copies(index):
        head = index * GROUP
        cols = pl.ds(head * nope, GROUP * nope)
        part = pl.ds(head, GROUP)
        return [
            pltpu.make_async_copy(qn_hbm.at[:, cols], qn_ref.at[:, cols], sems.at[index, 0]),
            pltpu.make_async_copy(ku_hbm.at[part], ku_ref.at[part], sems.at[index, 1]),
        ]

    rope_copy = pltpu.make_async_copy(qr_hbm, qr_ref, sems.at[groups, 0])
    lengths_copy = pltpu.make_async_copy(lengths_hbm, lengths_ref, sems.at[groups, 1])
    lengths_copy.start()
    rope_copy.start()
    for index in range(groups):
        for copy in copies(index):
            copy.start()
    lengths_copy.wait()
    ctx = lax.axis_index("ctx")
    freq = frequencies(rope, (8, 128))[0:1, :]
    key_rows = rows // 2
    for plane in range(3):
        first = half_start(plane, False, False, False, rows, key_rows)
        pos = first + lax.broadcasted_iota(jnp.int32, (key_rows, 128), 0)
        angle = (pos - begin_of(pos, lengths_ref)).astype(jnp.float32) * freq
        cos_ref[plane] = jnp.cos(angle)
        sin_ref[plane] = jnp.sin(angle)
    pos = ctx * rows + lax.broadcasted_iota(jnp.int32, (rows, 128), 0)
    angle = (pos - begin_of(pos, lengths_ref)).astype(jnp.float32) * freq
    lane = lax.broadcasted_iota(jnp.int32, (rows, 128), 1)
    low = lax.rem(lane, rope) < rope // 2
    cos = jnp.cos(angle)
    sin = jnp.sin(angle)
    sin = jnp.where(low, -sin, sin)
    rope_copy.wait()
    for index in range(groups):
        for copy in copies(index):
            copy.wait()
        for head in range(index * GROUP, (index + 1) * GROUP, 2):
            pair = qr_ref[:, head * rope : (head + 2) * rope].astype(jnp.float32)
            partner = jnp.where(low, pltpu.roll(pair, 128 - rope // 2, 1), pltpu.roll(pair, rope // 2, 1))
            rotated = pair * cos + partner * sin
            for k, part in enumerate((rotated, pltpu.roll(rotated, rope, 1))):
                at = slice((head + k) * rows, (head + k + 1) * rows)
                nope_rows = qn_ref[:, (head + k) * nope : (head + k + 1) * nope]
                absorbed = jnp.dot(nope_rows, ku_ref[head + k], preferred_element_type=jnp.float32)
                q_ref[at, :latent] = absorbed.astype(jnp.bfloat16)
                q_ref[at, latent:] = jnp.where(lane < rope, part, 0.0).astype(jnp.bfloat16)


def rows_kernel(own_ref, one_ref, two_ref, gain_ref, cos_ref, sin_ref, rows_ref, send_ref):
    latent = gain_ref.shape[1]
    full = own_ref.shape[1]
    half = (full - latent) // 2
    row = lax.rem(lax.axis_index("ctx") // 2, 2)
    gain = gain_ref[0:1, :]
    for plane, raw_ref in enumerate((own_ref, one_ref, two_ref)):
        part = raw_ref[:, :latent].astype(jnp.float32)
        mean = jnp.mean(part * part, axis=1, keepdims=True)
        normed = part * lax.rsqrt(mean + epsilon) * gain
        rope = raw_ref[:, latent:].astype(jnp.float32)
        first, second = rope[:, :half], rope[:, half:]
        cos, sin = cos_ref[plane][:, :half], sin_ref[plane][:, :half]
        turned = jnp.concatenate([first * cos - second * sin, second * cos + first * sin], axis=1)
        rows_ref[plane, :, :latent] = normed.astype(jnp.bfloat16)
        rows_ref[plane, :, latent:] = turned.astype(jnp.bfloat16)
    send_ref[...] = rows_ref[pl.ds(row, 2)]


def widen(column, count):
    return jnp.concatenate([column] * count, axis=1)


def value_heads(base, mixed, vu_ref, held_ref, out_ref, sems):
    value = vu_ref.shape[2]
    rows = held_ref.shape[0]
    for j in range(SUB):
        cols = slice((base + j) * value, (base + j + 1) * value)
        result = jnp.dot(mixed[j * rows : (j + 1) * rows], vu_ref[base + j], preferred_element_type=jnp.float32)
        held_ref[:, cols] = result.astype(jnp.bfloat16)
    if (base + SUB) % VALUE_GROUP:
        return []
    group = base // VALUE_GROUP
    cols = slice(group * VALUE_GROUP * value, (base + SUB) * value)
    copy = pltpu.make_async_copy(held_ref.at[:, cols], out_ref.at[:, cols], sems.at[group])
    copy.start()
    return [copy]


def attend_kernel(layout, scale, first_call, last_call, lengths_ref, q_ref, *refs):
    count = len(layout)
    piece_refs, refs = refs[:count], refs[count:]
    if not first_call:
        sum_in, most_in, total_in = refs[:3]
        refs = refs[3:]
    if last_call:
        vu_ref, out_ref, held_ref, sems, kv_ref = refs
        latent = vu_ref.shape[1]
    else:
        sum_out, most_out, total_out, kv_ref = refs
        latent = sum_out.shape[1]
    half_rows = piece_refs[0].shape[1]
    rows = 2 * half_rows
    heads = q_ref.shape[0] // rows
    ctx = lax.axis_index("ctx")
    core = lax.rem(ctx, 2)
    row = lax.rem(ctx // 2, 2)
    keys = kv_ref.shape[0]
    full = piece_refs[0].shape[2]
    kv_ref[:, full:] = jnp.zeros((keys, kv_ref.shape[1] - full), jnp.bfloat16)
    firsts = []
    for step in range(2):
        for (flip_y, flip_core, flip_head), ref in zip(layout, piece_refs):
            if flip_y:
                index, plane = 0, 1 - row
            else:
                index = plane = 1 - core if flip_core else 0
            at = len(firsts) * half_rows
            kv_ref[at : at + half_rows, :full] = ref[index + step]
            firsts.append(half_start(plane + step, flip_y, flip_core, flip_head, rows, half_rows))
    earliest = begin_of(ctx * rows, lengths_ref)
    older_live = functools.reduce(jnp.maximum, firsts[count:]) + half_rows > earliest
    exponent = scale * math.log2(math.e)

    def span(base):
        return slice(base * rows, (base + SUB) * rows)

    def visit(pieces):
        width = pieces * half_rows
        lane = lax.broadcasted_iota(jnp.int32, (rows, width), 1)
        key_pos = lane + firsts[0]
        for piece in range(1, pieces):
            at = piece * half_rows
            key_pos = jnp.where(lane >= at, lane + (firsts[piece] - at), key_pos)
        pos = ctx * rows + lax.broadcasted_iota(jnp.int32, (rows, width), 0)
        live = (key_pos <= pos) & (key_pos >= begin_of(pos, lengths_ref))

        def scores(base):
            return lax.dot_general(
                q_ref[span(base), :], kv_ref[:width, :], (((1,), (1,)), ((), ())), preferred_element_type=jnp.float32
            )

        def finish(base, weights, total, most, factor):
            mixed = jnp.dot(weights, kv_ref[:width, :latent], preferred_element_type=jnp.float32)
            if not first_call:
                total = total + factor * total_in[span(base), :]
                mixed = mixed + widen(factor, latent // 128) * sum_in[span(base), :]
            if last_call:
                mixed = mixed * widen(1.0 / total, latent // 128)
                copies.extend(value_heads(base, mixed.astype(jnp.bfloat16), vu_ref, held_ref, out_ref, sems))
            else:
                sum_out[span(base), :] = mixed
                most_out[span(base), :] = most
                total_out[span(base), :] = total

        copies = []
        now = scores(0)
        waiting = None
        for base in range(0, heads, SUB):
            later = scores(base + SUB) if base + SUB < heads else None
            now = jnp.where(live[None], now.reshape(SUB, rows, width), masked_score).reshape(SUB * rows, width)
            most = jnp.broadcast_to(jnp.max(now, axis=1, keepdims=True), (SUB * rows, 128))
            factor = None
            if not first_call:
                before = most_in[span(base), :]
                most = jnp.maximum(most, before)
                factor = jnp.exp2((before - most) * exponent)
            weights = jnp.exp2((now - widen(most, width // 128)) * exponent)
            total = jnp.broadcast_to(jnp.sum(weights, axis=1, keepdims=True), (SUB * rows, 128))
            if waiting:
                finish(*waiting)
            waiting = (base, weights.astype(jnp.bfloat16), total, most, factor)
            now = later
        finish(*waiting)
        for copy in copies:
            copy.wait()

    @pl.when(older_live)
    def all_pieces():
        visit(2 * count)

    @pl.when(jnp.logical_not(older_live))
    def newer_pieces():
        visit(count)


def params(limit=24):
    return pltpu.CompilerParams(vmem_limit_bytes=limit * 2**20)


def shards(latent_raw, kv_gain, query_nope, query_rope, key_up, value_up, doc_lengths):
    rows = query_nope.shape[0]
    heads, nope, latent = key_up.shape
    value = value_up.shape[2]
    half_rows, full = latent_raw.shape
    rope = full - latent
    wide = latent + 128
    ctx_size = lax.axis_size("ctx")
    scale = (nope + rope) ** (-0.5)

    def plane_shift(array, planes):
        steps = planes * PLANE
        return lax.ppermute(array, "ctx", [(s, (s + steps) % ctx_size) for s in range(ctx_size)])

    def swap_ctx(array, bit):
        return lax.ppermute(array, "ctx", [(s, s ^ bit) for s in range(ctx_size)])

    def swap_head(array):
        return lax.ppermute(array, "head", [(0, 1), (1, 0)])

    one = plane_shift(latent_raw, 1)
    two = plane_shift(latent_raw, 2)
    table = jax.ShapeDtypeStruct((3, half_rows, 128), jnp.float32)
    queries, cos, sin = pl.pallas_call(
        query_kernel,
        out_shape=(jax.ShapeDtypeStruct((heads * rows, wide), jnp.bfloat16), table, table),
        in_specs=[HBM] * 4,
        out_specs=[VMEM] * 3,
        scratch_shapes=[
            pltpu.VMEM(query_nope.shape, jnp.bfloat16),
            pltpu.VMEM(query_rope.shape, jnp.bfloat16),
            pltpu.VMEM(key_up.shape, jnp.bfloat16),
            pltpu.SMEM(doc_lengths.shape, jnp.int32),
            pltpu.SemaphoreType.DMA((heads // GROUP + 1, 2)),
        ],
        compiler_params=params(),
        cost_estimate=pl.CostEstimate(
            flops=2 * heads * rows * nope * latent, bytes_accessed=8 * 2**20, transcendentals=0
        ),
        name="queries",
    )(
        *(pltpu.with_memory_space_constraint(array, pltpu.HBM) for array in (doc_lengths, query_nope, query_rope, key_up))
    )
    near, send = pl.pallas_call(
        rows_kernel,
        out_shape=(
            jax.ShapeDtypeStruct((3, half_rows, full), jnp.bfloat16),
            jax.ShapeDtypeStruct((2, half_rows, full), jnp.bfloat16),
        ),
        in_specs=[VMEM] * 6,
        out_specs=[VMEM] * 2,
        compiler_params=params(),
        name="rows",
    )(latent_raw, one, two, kv_gain[None], cos, sin)
    across = swap_ctx(send, 2)
    side = swap_head(near)
    near_pieces = [(near, (False, False, False)), (swap_ctx(near, 1), (False, True, False))]

    state_shape = (
        jax.ShapeDtypeStruct((heads * rows, latent), jnp.float32),
        jax.ShapeDtypeStruct((heads * rows, 128), jnp.float32),
        jax.ShapeDtypeStruct((heads * rows, 128), jnp.float32),
    )
    names = iter(("attend_near", "attend_across", "attend_far"))

    def attend(part, state, last=False):
        pieces, layout = zip(*part)
        keys = 2 * half_rows * len(pieces)
        scratch = [pltpu.VMEM((keys, wide), jnp.bfloat16)]
        if last:
            scratch = [
                pltpu.VMEM((rows, heads * value), jnp.bfloat16),
                pltpu.SemaphoreType.DMA((heads // VALUE_GROUP,)),
            ] + scratch
        extra = (value_up,) if last else ()
        return pl.pallas_call(
            functools.partial(attend_kernel, layout, scale, not state, last),
            out_shape=jax.ShapeDtypeStruct((rows, heads * value), jnp.bfloat16) if last else state_shape,
            in_specs=[SMEM] + [VMEM] * (1 + len(pieces) + len(state) + len(extra)),
            out_specs=HBM if last else [VMEM] * 3,
            scratch_shapes=scratch,
            compiler_params=params(18 if last else 8),
            name=next(names),
        )(doc_lengths, queries, *pieces, *state, *extra)

    state = attend(near_pieces, ())
    across, *state = lax.optimization_barrier((across, *state))
    corner = swap_head(across)
    across_pieces = [(across, (True, False, False)), (swap_ctx(across, 1), (True, True, False))]
    state = attend(across_pieces, state)
    side, corner, *state = lax.optimization_barrier((side, corner, *state))
    side_pieces = [(side, (False, False, True)), (swap_ctx(side, 1), (False, True, True))]
    corner_pieces = [(corner, (True, False, True)), (swap_ctx(corner, 1), (True, True, True))]
    return attend(side_pieces + corner_pieces, state, last=True)


def solution(mesh):
    return jax.shard_map(
        shards,
        mesh=mesh,
        in_specs=(
            P(("ctx", "head"), None),
            P(),
            P("ctx", "head"),
            P("ctx", "head"),
            P("head", None, None),
            P("head", None, None),
            P(),
        ),
        out_specs=P("ctx", "head"),
        check_vma=False,
    )
```

```python
import functools
import math

import jax
import jax.numpy as jnp
import numpy as np
from jax import lax
from jax.experimental import pallas as pl
from jax.experimental.pallas import tpu as pltpu
from jax.sharding import PartitionSpec as P

epsilon = 1e-06
masked_score = -1e30
PLANE = 4
GROUP = 8
SUB = 4
VALUE_GROUP = 4
HBM = pl.BlockSpec(memory_space=pltpu.HBM)
VMEM = pl.BlockSpec(memory_space=pltpu.VMEM)
SMEM = pl.BlockSpec(memory_space=pltpu.SMEM)


def begin_of(positions, lengths_ref):
    begin = jnp.zeros_like(positions)
    start = jnp.int32(0)
    for doc in range(lengths_ref.shape[0] - 1):
        start = start + lengths_ref[doc]
        begin = jnp.where(positions >= start, start, begin)
    return begin


def half_start(plane, flip_y, flip_core, flip_head, block_rows, half_rows):
    ctx = lax.axis_index("ctx")
    head = lax.axis_index("head")
    core = lax.rem(ctx, 2)
    row = lax.rem(ctx // 2, 2)
    base = ctx // PLANE - plane
    row = 1 - row if flip_y else row
    core = 1 - core if flip_core else core
    head = 1 - head if flip_head else head
    return (base * PLANE + row * 2 + core) * block_rows + head * half_rows


def frequencies(rope, shape):
    half = rope // 2
    exponents = np.float32(-2.0) * np.arange(half, dtype=np.float32) / np.float32(rope)
    values = np.float32(10000.0) ** exponents
    lane = lax.rem(lax.broadcasted_iota(jnp.int32, shape, 1), half)
    freq = jnp.zeros(shape, jnp.float32)
    for index in range(half):
        freq = jnp.where(lane == index, float(values[index]), freq)
    return freq


def query_kernel(lengths_hbm, qn_hbm, qr_hbm, ku_hbm, q_ref, cos_ref, sin_ref, qn_ref, qr_ref, ku_ref, lengths_ref, sems):
    rows = qn_ref.shape[0]
    heads, nope, latent = ku_ref.shape
    rope = qr_ref.shape[1] // heads
    groups = heads // GROUP

    def copies(index):
        head = index * GROUP
        cols = pl.ds(head * nope, GROUP * nope)
        part = pl.ds(head, GROUP)
        return [
            pltpu.make_async_copy(qn_hbm.at[:, cols], qn_ref.at[:, cols], sems.at[index, 0]),
            pltpu.make_async_copy(ku_hbm.at[part], ku_ref.at[part], sems.at[index, 1]),
        ]

    rope_copy = pltpu.make_async_copy(qr_hbm, qr_ref, sems.at[groups, 0])
    lengths_copy = pltpu.make_async_copy(lengths_hbm, lengths_ref, sems.at[groups, 1])
    lengths_copy.start()
    rope_copy.start()
    for index in range(groups):
        for copy in copies(index):
            copy.start()
    lengths_copy.wait()
    ctx = lax.axis_index("ctx")
    freq = frequencies(rope, (8, 128))[0:1, :]
    key_rows = rows // 2
    for plane in range(3):
        first = half_start(plane, False, False, False, rows, key_rows)
        pos = first + lax.broadcasted_iota(jnp.int32, (key_rows, 128), 0)
        angle = (pos - begin_of(pos, lengths_ref)).astype(jnp.float32) * freq
        cos_ref[plane] = jnp.cos(angle)
        sin_ref[plane] = jnp.sin(angle)
    pos = ctx * rows + lax.broadcasted_iota(jnp.int32, (rows, 128), 0)
    angle = (pos - begin_of(pos, lengths_ref)).astype(jnp.float32) * freq
    lane = lax.broadcasted_iota(jnp.int32, (rows, 128), 1)
    low = lax.rem(lane, rope) < rope // 2
    cos = jnp.cos(angle)
    sin = jnp.sin(angle)
    sin = jnp.where(low, -sin, sin)
    rope_copy.wait()
    for index in range(groups):
        for copy in copies(index):
            copy.wait()
        for head in range(index * GROUP, (index + 1) * GROUP, 2):
            pair = qr_ref[:, head * rope : (head + 2) * rope].astype(jnp.float32)
            partner = jnp.where(low, pltpu.roll(pair, 128 - rope // 2, 1), pltpu.roll(pair, rope // 2, 1))
            rotated = pair * cos + partner * sin
            for k, part in enumerate((rotated, pltpu.roll(rotated, rope, 1))):
                at = slice((head + k) * rows, (head + k + 1) * rows)
                nope_rows = qn_ref[:, (head + k) * nope : (head + k + 1) * nope]
                absorbed = jnp.dot(nope_rows, ku_ref[head + k], preferred_element_type=jnp.float32)
                q_ref[at, :latent] = absorbed.astype(jnp.bfloat16)
                q_ref[at, latent:] = jnp.where(lane < rope, part, 0.0).astype(jnp.bfloat16)


def rows_kernel(own_ref, one_ref, two_ref, gain_ref, cos_ref, sin_ref, rows_ref, send_ref):
    latent = gain_ref.shape[1]
    full = own_ref.shape[1]
    half = (full - latent) // 2
    row = lax.rem(lax.axis_index("ctx") // 2, 2)
    gain = gain_ref[0:1, :]
    for plane, raw_ref in enumerate((own_ref, one_ref, two_ref)):
        part = raw_ref[:, :latent].astype(jnp.float32)
        mean = jnp.mean(part * part, axis=1, keepdims=True)
        normed = part * lax.rsqrt(mean + epsilon) * gain
        rope = raw_ref[:, latent:].astype(jnp.float32)
        first, second = rope[:, :half], rope[:, half:]
        cos, sin = cos_ref[plane][:, :half], sin_ref[plane][:, :half]
        turned = jnp.concatenate([first * cos - second * sin, second * cos + first * sin], axis=1)
        rows_ref[plane, :, :latent] = normed.astype(jnp.bfloat16)
        rows_ref[plane, :, latent:] = turned.astype(jnp.bfloat16)
    send_ref[...] = rows_ref[pl.ds(row, 2)]


def widen(column, count):
    return jnp.concatenate([column] * count, axis=1)


def value_heads(base, mixed, vu_ref, held_ref, out_ref, sems):
    value = vu_ref.shape[2]
    rows = held_ref.shape[0]
    for j in range(SUB):
        cols = slice((base + j) * value, (base + j + 1) * value)
        result = jnp.dot(mixed[j * rows : (j + 1) * rows], vu_ref[base + j], preferred_element_type=jnp.float32)
        held_ref[:, cols] = result.astype(jnp.bfloat16)
    if (base + SUB) % VALUE_GROUP:
        return []
    group = base // VALUE_GROUP
    cols = slice(group * VALUE_GROUP * value, (base + SUB) * value)
    copy = pltpu.make_async_copy(held_ref.at[:, cols], out_ref.at[:, cols], sems.at[group])
    copy.start()
    return [copy]


def attend_kernel(layout, scale, first_call, last_call, lengths_ref, q_ref, *refs):
    count = len(layout)
    piece_refs, refs = refs[:count], refs[count:]
    if not first_call:
        sum_in, most_in, total_in = refs[:3]
        refs = refs[3:]
    if last_call:
        vu_ref, out_ref, held_ref, sems, kv_ref = refs
        latent = vu_ref.shape[1]
    else:
        sum_out, most_out, total_out, kv_ref = refs
        latent = sum_out.shape[1]
    half_rows = piece_refs[0].shape[1]
    rows = 2 * half_rows
    heads = q_ref.shape[0] // rows
    ctx = lax.axis_index("ctx")
    core = lax.rem(ctx, 2)
    row = lax.rem(ctx // 2, 2)
    keys = kv_ref.shape[0]
    full = piece_refs[0].shape[2]
    kv_ref[:, full:] = jnp.zeros((keys, kv_ref.shape[1] - full), jnp.bfloat16)
    firsts = []
    for step in range(2):
        for (flip_y, flip_core, flip_head), ref in zip(layout, piece_refs):
            if flip_y:
                index, plane = 0, 1 - row
            else:
                index = plane = 1 - core if flip_core else 0
            at = len(firsts) * half_rows
            kv_ref[at : at + half_rows, :full] = ref[index + step]
            firsts.append(half_start(plane + step, flip_y, flip_core, flip_head, rows, half_rows))
    earliest = begin_of(ctx * rows, lengths_ref)
    older_live = functools.reduce(jnp.maximum, firsts[count:]) + half_rows > earliest
    exponent = scale * math.log2(math.e)

    def span(base):
        return slice(base * rows, (base + SUB) * rows)

    def visit(pieces):
        width = pieces * half_rows
        lane = lax.broadcasted_iota(jnp.int32, (rows, width), 1)
        key_pos = lane + firsts[0]
        for piece in range(1, pieces):
            at = piece * half_rows
            key_pos = jnp.where(lane >= at, lane + (firsts[piece] - at), key_pos)
        pos = ctx * rows + lax.broadcasted_iota(jnp.int32, (rows, width), 0)
        live = (key_pos <= pos) & (key_pos >= begin_of(pos, lengths_ref))

        def scores(base):
            return lax.dot_general(
                q_ref[span(base), :], kv_ref[:width, :], (((1,), (1,)), ((), ())), preferred_element_type=jnp.float32
            )

        def finish(base, weights, total, most, factor):
            mixed = jnp.dot(weights, kv_ref[:width, :latent], preferred_element_type=jnp.float32)
            if not first_call:
                total = total + factor * total_in[span(base), :]
                mixed = mixed + widen(factor, latent // 128) * sum_in[span(base), :]
            if last_call:
                mixed = mixed * widen(1.0 / total, latent // 128)
                copies.extend(value_heads(base, mixed.astype(jnp.bfloat16), vu_ref, held_ref, out_ref, sems))
            else:
                sum_out[span(base), :] = mixed
                most_out[span(base), :] = most
                total_out[span(base), :] = total

        copies = []
        now = scores(0)
        waiting = None
        for base in range(0, heads, SUB):
            later = scores(base + SUB) if base + SUB < heads else None
            now = jnp.where(live[None], now.reshape(SUB, rows, width), masked_score).reshape(SUB * rows, width)
            most = jnp.broadcast_to(jnp.max(now, axis=1, keepdims=True), (SUB * rows, 128))
            factor = None
            if not first_call:
                before = most_in[span(base), :]
                most = jnp.maximum(most, before)
                factor = jnp.exp2((before - most) * exponent)
            weights = jnp.exp2((now - widen(most, width // 128)) * exponent)
            total = jnp.broadcast_to(jnp.sum(weights, axis=1, keepdims=True), (SUB * rows, 128))
            if waiting:
                finish(*waiting)
            waiting = (base, weights.astype(jnp.bfloat16), total, most, factor)
            now = later
        finish(*waiting)
        for copy in copies:
            copy.wait()

    @pl.when(older_live)
    def all_pieces():
        visit(2 * count)

    @pl.when(jnp.logical_not(older_live))
    def newer_pieces():
        visit(count)


def params(limit=24):
    return pltpu.CompilerParams(vmem_limit_bytes=limit * 2**20)


def shards(latent_raw, kv_gain, query_nope, query_rope, key_up, value_up, doc_lengths):
    rows = query_nope.shape[0]
    heads, nope, latent = key_up.shape
    value = value_up.shape[2]
    half_rows, full = latent_raw.shape
    rope = full - latent
    wide = latent + 128
    ctx_size = lax.axis_size("ctx")
    scale = (nope + rope) ** (-0.5)

    def plane_shift(array, planes):
        steps = planes * PLANE
        return lax.ppermute(array, "ctx", [(s, (s + steps) % ctx_size) for s in range(ctx_size)])

    def swap_ctx(array, bit):
        return lax.ppermute(array, "ctx", [(s, s ^ bit) for s in range(ctx_size)])

    def swap_head(array):
        return lax.ppermute(array, "head", [(0, 1), (1, 0)])

    one = plane_shift(latent_raw, 1)
    two = plane_shift(latent_raw, 2)
    table = jax.ShapeDtypeStruct((3, half_rows, 128), jnp.float32)
    queries, cos, sin = pl.pallas_call(
        query_kernel,
        out_shape=(jax.ShapeDtypeStruct((heads * rows, wide), jnp.bfloat16), table, table),
        in_specs=[HBM] * 4,
        out_specs=[VMEM] * 3,
        scratch_shapes=[
            pltpu.VMEM(query_nope.shape, jnp.bfloat16),
            pltpu.VMEM(query_rope.shape, jnp.bfloat16),
            pltpu.VMEM(key_up.shape, jnp.bfloat16),
            pltpu.SMEM(doc_lengths.shape, jnp.int32),
            pltpu.SemaphoreType.DMA((heads // GROUP + 1, 2)),
        ],
        compiler_params=params(),
        cost_estimate=pl.CostEstimate(
            flops=2 * heads * rows * nope * latent, bytes_accessed=8 * 2**20, transcendentals=0
        ),
        name="queries",
    )(
        *(pltpu.with_memory_space_constraint(array, pltpu.HBM) for array in (doc_lengths, query_nope, query_rope, key_up))
    )
    near, send = pl.pallas_call(
        rows_kernel,
        out_shape=(
            jax.ShapeDtypeStruct((3, half_rows, full), jnp.bfloat16),
            jax.ShapeDtypeStruct((2, half_rows, full), jnp.bfloat16),
        ),
        in_specs=[VMEM] * 6,
        out_specs=[VMEM] * 2,
        compiler_params=params(),
        name="rows",
    )(latent_raw, one, two, kv_gain[None], cos, sin)
    across = swap_ctx(send, 2)
    side = swap_head(near)
    near_pieces = [(near, (False, False, False)), (swap_ctx(near, 1), (False, True, False))]

    state_shape = (
        jax.ShapeDtypeStruct((heads * rows, latent), jnp.float32),
        jax.ShapeDtypeStruct((heads * rows, 128), jnp.float32),
        jax.ShapeDtypeStruct((heads * rows, 128), jnp.float32),
    )
    names = iter(("attend_near", "attend_across", "attend_far"))

    def attend(part, state, last=False):
        pieces, layout = zip(*part)
        keys = 2 * half_rows * len(pieces)
        scratch = [pltpu.VMEM((keys, wide), jnp.bfloat16)]
        if last:
            scratch = [
                pltpu.VMEM((rows, heads * value), jnp.bfloat16),
                pltpu.SemaphoreType.DMA((heads // VALUE_GROUP,)),
            ] + scratch
        extra = (value_up,) if last else ()
        return pl.pallas_call(
            functools.partial(attend_kernel, layout, scale, not state, last),
            out_shape=jax.ShapeDtypeStruct((rows, heads * value), jnp.bfloat16) if last else state_shape,
            in_specs=[SMEM] + [VMEM] * (1 + len(pieces) + len(state) + len(extra)),
            out_specs=HBM if last else [VMEM] * 3,
            scratch_shapes=scratch,
            compiler_params=params(18 if last else 8),
            name=next(names),
        )(doc_lengths, queries, *pieces, *state, *extra)

    state = attend(near_pieces, ())
    across, *state = lax.optimization_barrier((across, *state))
    corner = swap_head(across)
    across_pieces = [(across, (True, False, False)), (swap_ctx(across, 1), (True, True, False))]
    state = attend(across_pieces, state)
    side, corner, *state = lax.optimization_barrier((side, corner, *state))
    side_pieces = [(side, (False, False, True)), (swap_ctx(side, 1), (False, True, True))]
    corner_pieces = [(corner, (True, False, True)), (swap_ctx(corner, 1), (True, True, True))]
    return attend(side_pieces + corner_pieces, state, last=True)


def solution(mesh):
    return jax.shard_map(
        shards,
        mesh=mesh,
        in_specs=(
            P(("ctx", "head"), None),
            P(),
            P("ctx", "head"),
            P("ctx", "head"),
            P("head", None, None),
            P("head", None, None),
            P(),
        ),
        out_specs=P("ctx", "head"),
        check_vma=False,
    )
```
